256 devices in a mesh: gx: 8 (over y, core), gy: 32 (over x, z).
Axes of the slice: x: 4, y: 4, z: 8, core: 2. Of those that a mesh axis runs over, the one named last changes fastest.
Arguments:
- query: bfloat16 [192, 4, 64, 128], P(None, None, 'gx'), may hold values from -10 to 10
- cache_key: bfloat16 [192, 8, 2048, 128], P('gy', 'gx'), may hold values from -10 to 10
- cache_value: bfloat16 [192, 8, 2048, 128], P('gy', 'gx'), may hold values from -18 to 18
- new_key: bfloat16 [192, 4, 8, 128], P('gy', None, 'gx'), may hold values from -10 to 10
- new_value: bfloat16 [192, 4, 8, 128], P('gy', None, 'gx'), may hold values from -18 to 18
- prefix_len: int32 [192], replicated, may hold values from 1 to 2048, as said below
- residual: bfloat16 [768, 8192], P('gx', 'gy'), may hold values from -1.796875 to 1.796875
- out_weight: bfloat16 [8192, 8192], P('gx', 'gy'), may hold values from -0.0625 to 0.0625
- norm_gain: float32 [8192], replicated, may hold values from 0.1 to 1.9
- gate_weight: bfloat16 [8192, 28672], P('gx', 'gy'), may hold values from -0.0625 to 0.0625
- up_weight: bfloat16 [8192, 28672], P('gx', 'gy'), may hold values from -0.0625 to 0.0625
Outputs:
- stream: bfloat16 [768, 8192], P('gx', 'gy')
- activated: bfloat16 [768, 28672], P('gx', 'gy')
The draws below stay inside these ranges and needn't reach their ends.
Inputs may be any that keep to these rules, and one draw needn't show every extreme that they name: `prefix_len`: one rollout's prefix holds exactly 2048 live slots and another's exactly 1.
All inputs are finite; a program needn't handle non-finite values.
Results may differ from the reference program's by a relative error of at most 0.04.
Values may be sent and summed in bfloat16 or wider, within the bound.
A program may use at most 128 MiB of HBM per device.

```python
import jax
import jax.numpy as jnp
from jax import lax

D = 8192
FF = 28672
HEADS = 64
KVH = 8
HD = 128
NEW = 4
CACHE = 2048
GROUP = 8
ROLLOUTS = 192
TOKENS = 768


def draw_query(key, part):
    own_key = jax.random.fold_in(key, 11)
    shape = (ROLLOUTS, NEW, HEADS, HD)
    values = jax.random.truncated_normal(own_key, -6.0, 6.0, shape, jnp.float32)
    return values.astype(jnp.bfloat16)


def draw_cache_key(key, part):
    own_key = jax.random.fold_in(key, 23)
    shape = (ROLLOUTS, KVH, CACHE, HD)
    values = jax.random.truncated_normal(own_key, -6.0, 6.0, shape, jnp.float32)
    return values.astype(jnp.bfloat16)


def draw_new_key(key, part):
    own_key = jax.random.fold_in(key, 37)
    shape = (ROLLOUTS, NEW, KVH, HD)
    values = jax.random.truncated_normal(own_key, -6.0, 6.0, shape, jnp.float32)
    return values.astype(jnp.bfloat16)


def draw_prefix_len(key, part):
    own_key = jax.random.fold_in(key, 41)
    first, second, third, fourth = jax.random.split(own_key, 4)
    left = jax.random.randint(first, (ROLLOUTS,), 0, CACHE, jnp.int32)
    right = jax.random.randint(second, (ROLLOUTS,), 0, CACHE, jnp.int32)
    lengths = CACHE - left * right // CACHE
    longest = jax.random.randint(third, (), 0, ROLLOUTS, jnp.int32)
    shortest = (longest + 1 + jax.random.randint(fourth, (), 0, ROLLOUTS - 1, jnp.int32)) % ROLLOUTS
    lengths = lengths.at[longest].set(CACHE)
    lengths = lengths.at[shortest].set(1)
    return lengths


def block_scale(key, extent, cuts, least, top_value):
    factor_of, own = 1.0, jax.random.fold_in(key, 6)
    for axis_at, parts in cuts:
        heights = jnp.exp(jax.random.uniform(jax.random.fold_in(own, axis_at), (parts,), jnp.float32, least / len(cuts), top_value / len(cuts)))
        factor_of = factor_of * jnp.repeat(heights, extent[axis_at] // parts).reshape([-1 if axis == axis_at else 1 for axis in range(len(extent))])
    return factor_of


def noise(stream_key, extent, width, reach, cuts=(), kind=jnp.bfloat16):
    entries = jax.random.normal(stream_key, extent, jnp.float32) * width
    if len(cuts) > 0:
        entries = block_scale(stream_key, extent, cuts, -0.22, 0.18) * entries
    return jnp.clip(entries, min=-reach, max=reach).astype(kind)


def setup_inputs(seed: int = 0) -> dict:
    key_of = jax.random.split(jax.random.key(seed), 12)
    query = draw_query(jax.random.fold_in(key_of[11], 71), 0)
    cache_key = draw_cache_key(jax.random.fold_in(key_of[11], 71), 0)
    cache_value = noise(key_of[2], (ROLLOUTS, KVH, CACHE, HD), 3.0, 18.0, ((0, 32), (1, 8)))
    new_key = draw_new_key(jax.random.fold_in(key_of[11], 71), 0)
    new_value = noise(key_of[4], (ROLLOUTS, NEW, KVH, HD), 3.0, 18.0, ((0, 32), (2, 8)))
    prefix_len = draw_prefix_len(jax.random.fold_in(key_of[11], 71), 0)
    residual = noise(key_of[6], (TOKENS, D), 0.3, 1.796875, ((0, 8), (1, 32)))
    out_weight = noise(key_of[7], (D, D), D ** -0.5, 0.0625, ((0, 8), (1, 32)))
    norm_gain = jnp.clip(1.0 + 0.18 * jax.random.normal(key_of[8], (D,), jnp.float32), 0.1, 1.9)
    gate_weight = noise(key_of[9], (D, FF), D ** -0.5, 0.0625, ((0, 8), (1, 32)))
    up_weight = noise(key_of[10], (D, FF), D ** -0.5, 0.0625, ((0, 8), (1, 32)))
    return {"query": query, "cache_key": cache_key, "cache_value": cache_value, "new_key": new_key, "new_value": new_value, "prefix_len": prefix_len, "residual": residual, "out_weight": out_weight, "norm_gain": norm_gain, "gate_weight": gate_weight, "up_weight": up_weight}


masked_score = -1e+30
norm_eps = 1e-05

def attend(items):
    q_rows, keys, values, fresh_keys, fresh_values, length = items
    scale = HD ** (-0.5)
    queries = q_rows.reshape(NEW, KVH, GROUP, HD)
    cached = jnp.einsum('tkgd,kpd->kgtp', queries.astype(jnp.float32), keys.astype(jnp.float32), precision=lax.Precision.HIGHEST) * scale
    cached = jnp.where(jnp.arange(CACHE, dtype=jnp.int32) < length, cached, masked_score)
    fresh = jnp.einsum('tkgd,skd->kgts', queries.astype(jnp.float32), fresh_keys.astype(jnp.float32), precision=lax.Precision.HIGHEST) * scale
    causal = jnp.arange(NEW)[None, :] <= jnp.arange(NEW)[:, None]
    fresh = jnp.where(causal, fresh, masked_score)
    top = jnp.maximum(cached.max(-1), fresh.max(-1))
    cached_w = jnp.exp(cached - top[..., None])
    fresh_w = jnp.exp(fresh - top[..., None])
    total = cached_w.sum(-1) + fresh_w.sum(-1)
    cached_r = lax.optimization_barrier(cached_w.astype(jnp.bfloat16)).astype(jnp.float32)
    fresh_r = lax.optimization_barrier(fresh_w.astype(jnp.bfloat16)).astype(jnp.float32)
    mixed = jnp.einsum('kgtp,kpd->kgtd', cached_r, values.astype(jnp.float32), precision=lax.Precision.HIGHEST)
    mixed = mixed + jnp.einsum('kgts,skd->kgtd', fresh_r, fresh_values.astype(jnp.float32), precision=lax.Precision.HIGHEST)
    result = mixed / total[..., None]
    return result.transpose(2, 0, 1, 3).reshape(NEW, HEADS * HD)

def reference(query, cache_key, cache_value, new_key, new_value, prefix_len, residual, out_weight, norm_gain, gate_weight, up_weight):
    heads = lax.map(attend, (query, cache_key, cache_value, new_key, new_value, prefix_len))
    heads = heads.reshape(TOKENS, D).astype(jnp.bfloat16)
    projected = jnp.dot(heads, out_weight, preferred_element_type=jnp.float32)
    stream = (residual.astype(jnp.float32) + projected).astype(jnp.bfloat16)
    rows = stream.astype(jnp.float32)
    normed = (rows * lax.rsqrt(lax.optimization_barrier(jnp.mean(rows * rows, axis=-1, keepdims=True)) + norm_eps) * norm_gain).astype(jnp.bfloat16)
    gate = jnp.dot(normed, gate_weight, preferred_element_type=jnp.float32)
    up = jnp.dot(normed, up_weight, preferred_element_type=jnp.float32)
    activated = (jax.nn.silu(gate) * up).astype(jnp.bfloat16)
    return (stream, activated)
```

```python
import jax
import jax.numpy as jnp
from jax import lax
from jax.experimental import pallas as pl
from jax.experimental.pallas import tpu as pltpu
from jax.sharding import PartitionSpec as P

MESH = pl.DeviceIdType.MESH
F32 = jnp.float32
BF16 = jnp.bfloat16

NX, NY, NZ, NC = 4, 4, 8, 2
ROLLS = 6
NEW = 4
GROUP = 8
HD = 128
CACHE = 2048
ROWS = 96
COLS = 256
FEAT = 1024
HID = 896
TILE = 128
CHUNKS = HID // TILE
D = 8192
SPLIT = 48
masked_score = -1e30
norm_eps = 1e-05
LAG = 2


def layer_kernel(
    len_ref,
    q_hbm,
    k_hbm,
    v_hbm,
    nk_hbm,
    nv_hbm,
    res_hbm,
    ow_hbm,
    gain_hbm,
    gw_hbm,
    uw_hbm,
    stream_hbm,
    act_hbm,
    q_v,
    k_v,
    v_v,
    nk_v,
    nv_v,
    res_v,
    ow_v,
    gain_v,
    w_v,
    ho,
    g1,
    g2,
    p1,
    r1,
    st_v,
    h_v,
    sx,
    sz,
    x_other,
    x_own,
    cp_s,
    cp_r,
    own,
    y_s,
    y_r,
    act_v,
    kv_sem,
    in_sem,
    w_sem,
    ag_send,
    ag_recv,
    r1_send,
    r1_recv,
    perm_sem,
    sx_sem,
    sz_sem,
    cp_sem,
    ys_sem,
    yr_sem,
    out_sem,
):
    gx = lax.axis_index("gx")
    gy = lax.axis_index("gy")
    y, c = lax.div(gx, NC), lax.rem(gx, NC)
    x, z = lax.div(gy, NZ), lax.rem(gy, NZ)

    def at_x(d):
        return (gx, lax.rem(x + d, NX) * NZ + z)

    def at_z(d):
        return (gx, x * NZ + lax.rem(z + d + NZ, NZ))

    def at_y(d):
        return (lax.rem(y + d, NY) * NC + c, gy)

    def slot(dx, dz):
        return lax.rem(x + dx, NX) * NZ + lax.rem(z + dz + NZ, NZ)

    partner = (y * NC + 1 - c, gy)
    perm = (lax.div(gy, 4), 4 * gx + lax.rem(gy, 4))
    moves = jnp.logical_or(perm[0] != gx, perm[1] != gy)

    barrier = pltpu.get_barrier_semaphore()

    def greet(device):
        pl.semaphore_signal(barrier, inc=1, device_id=device, device_id_type=MESH)

    for d in range(1, NX):
        greet(at_x(d))
    for d in range(1, NZ):
        greet(at_z(d))
    for d in range(1, NY * NC):
        greet((lax.rem(gx + d, NY * NC), gy))

    @pl.when(moves)
    def _():
        greet(perm)

    def local(src, dst, sem):
        return pltpu.make_async_copy(src, dst, sem)

    small = [
        local(q_hbm.at[pl.ds(gy * ROLLS, ROLLS)], q_v, in_sem.at[0]),
        local(nk_hbm, nk_v, in_sem.at[1]),
        local(nv_hbm, nv_v, in_sem.at[2]),
    ]
    for copy in small:
        copy.start()
    kcopy = [local(k_hbm.at[r, 0], k_v.at[r], kv_sem.at[0, r]) for r in range(ROLLS)]
    vcopy = [local(v_hbm.at[r, 0], v_v.at[r], kv_sem.at[1, r]) for r in range(ROLLS)]
    for r in range(ROLLS):
        kcopy[r].start()
        vcopy[r].start()
    later = [
        local(ow_hbm, ow_v, in_sem.at[3]),
        local(res_hbm, res_v, in_sem.at[4]),
        local(gain_hbm, gain_v, in_sem.at[5]),
    ]
    for copy in later:
        copy.start()
    wcopy = []
    for j in range(CHUNKS):
        cols = pl.ds(j * TILE, TILE)
        wcopy.append(local(gw_hbm.at[:, cols], w_v.at[j, :, pl.ds(0, TILE)], w_sem.at[0, j]))
        wcopy.append(local(uw_hbm.at[:, cols], w_v.at[j, :, pl.ds(TILE, TILE)], w_sem.at[1, j]))
    for copy in wcopy:
        copy.start()

    for copy in small:
        copy.wait()
    place = lax.broadcasted_iota(jnp.int32, (NEW * GROUP, CACHE), 1)
    row_id = lax.broadcasted_iota(jnp.int32, (NEW * GROUP, 1), 0)
    scale = HD ** (-0.5)
    for r in range(ROLLS):
        kcopy[r].wait()
        q32 = q_v[r].astype(F32).reshape(NEW * GROUP, HD)
        nk32 = nk_v[r].astype(F32)
        nv32 = nv_v[r].astype(F32)
        scores = (
            lax.dot_general(
                q32.astype(BF16), k_v[r], (((1,), (1,)), ((), ())), preferred_element_type=F32
            )
            * scale
        )
        length = len_ref[gy * ROLLS + r]
        scores = jnp.where(place < length, scores, masked_score)
        fresh = []
        for s in range(NEW):
            one = jnp.sum(q32 * nk32[s : s + 1, :], axis=1, keepdims=True) * scale
            fresh.append(jnp.where(row_id >= s * GROUP, one, masked_score))
        top = jnp.max(scores, axis=1, keepdims=True)
        for s in range(NEW):
            top = jnp.maximum(top, fresh[s])
        weights = jnp.exp(scores - top)
        total = jnp.sum(weights, axis=1, keepdims=True)
        vcopy[r].wait()
        mixed = jnp.dot(weights.astype(BF16), v_v[r], preferred_element_type=F32)
        for s in range(NEW):
            weight = jnp.exp(fresh[s] - top)
            total = total + weight
            mixed = mixed + weight.astype(BF16).astype(F32) * nv32[s : s + 1, :]
        ho[pl.ds(r * NEW * GROUP, NEW * GROUP), :] = mixed / total

    slabs = []
    for q in range(4):
        parts = [ho[pl.ds(2 * q + h, ROLLS * NEW, stride=GROUP), :] for h in range(2)]
        slabs.append(jnp.concatenate(parts, axis=1))
    g1[gy] = jnp.concatenate(slabs, axis=0).astype(BF16)

    peers = NX - 1 + NZ - 1 + NY * NC - 1

    @pl.when(moves)
    def _():
        pl.semaphore_wait(barrier, peers + 1)

    @pl.when(jnp.logical_not(moves))
    def _():
        pl.semaphore_wait(barrier, peers)

    part_rows = (pl.ds(0, SPLIT), pl.ds(SPLIT, ROWS - SPLIT))

    def gather(ref, phase):
        sent = []

        def send(part, origin, device):
            block = ref.at[origin, part_rows[part]]
            copy = pltpu.make_async_remote_copy(
                src_ref=block,
                dst_ref=block,
                send_sem=ag_send.at[phase, len(sent)],
                recv_sem=ag_recv.at[phase, part, origin],
                device_id=device,
                device_id_type=MESH,
            )
            copy.start()
            sent.append(copy)

        def arrive(part, origin):
            block = ref.at[origin, part_rows[part]]
            local(block, block, ag_recv.at[phase, part, origin]).wait()

        mine = slot(0, 0)
        send(0, mine, at_z(1))
        send(0, mine, at_z(-1))
        for d in (1, 3, 2):
            send(1, mine, at_x(d))
        send(1, mine, at_z(1))
        send(1, mine, at_z(-1))
        for d in (1, 3, 2):
            send(0, mine, at_x(d))
        for s in range(1, 5):
            up, down = slot(0, -s), slot(0, s)
            arrive(0, up)
            if s < 4:
                send(0, up, at_z(1))
            for d in (1, 3, 2):
                send(0, up, at_x(d))
            if s < 4:
                arrive(0, down)
                if s < 3:
                    send(0, down, at_z(-1))
                for d in (1, 3, 2):
                    send(0, down, at_x(d))
            for d in (0, 1, 3, 2):
                if s == 1 and d > 0:
                    here = slot(d, 0)
                    arrive(1, here)
                    send(1, here, at_z(1))
                    send(1, here, at_z(-1))
            for d in (0, 1, 3, 2):
                if s < 4:
                    up = slot(d, -s)
                    arrive(1, up)
                    if s < 3:
                        send(1, up, at_z(1))
                down = slot(d, s)
                arrive(1, down)
                if s < 4:
                    send(1, down, at_z(-1))
        for s in range(NZ):
            for d in (1, 3, 2):
                arrive(0, slot(d, s))
        return sent

    sent = gather(g1, 0)

    for copy in later:
        copy.wait()

    def project(i):
        got = g1[pl.ds(4 * i, 4)].astype(F32)
        slabs = [got[:, 24 * q : 24 * q + 24, :].reshape(ROWS, COLS) for q in range(4)]
        block = jnp.concatenate(slabs, axis=1).astype(BF16)
        return jnp.dot(block, ow_v[...], preferred_element_type=F32).astype(BF16)

    def r1_copy(step):
        i = lax.rem(gx + 1 + step, NY * NC)
        return pltpu.make_async_remote_copy(
            src_ref=p1.at[step],
            dst_ref=r1.at[6 - step],
            send_sem=r1_send.at[step],
            recv_sem=r1_recv.at[6 - step],
            device_id=(i, gy),
            device_id_type=MESH,
        )

    def project_step(step, carry):
        p1[step] = project(lax.rem(gx + 1 + step, NY * NC))
        r1_copy(step).start()
        return carry

    lax.fori_loop(0, NY * NC - 1, project_step, 0)
    summed = res_v[...].astype(F32) + project(gx).astype(F32)
    for t in range(NY * NC - 1):
        local(r1.at[t], r1.at[t], r1_recv.at[t]).wait()
        summed = summed + r1[t].astype(F32)
    stream = summed.astype(BF16)
    st_v[...] = stream
    stream_out = local(st_v, stream_hbm, out_sem.at[0])
    stream_out.start()
    stream32 = stream.astype(F32)
    gain = jnp.concatenate(
        [gain_v[pl.ds(2 * gy, 1), :], gain_v[pl.ds(2 * gy + 1, 1), :]], axis=1
    )
    h_v[...] = (stream32 * gain).astype(BF16)

    perm_copy = pltpu.make_async_remote_copy(
        src_ref=h_v,
        dst_ref=g2.at[perm[1]],
        send_sem=perm_sem.at[0],
        recv_sem=perm_sem.at[1],
        device_id=perm,
        device_id_type=MESH,
    )

    @pl.when(moves)
    def _():
        perm_copy.start()

    @pl.when(jnp.logical_not(moves))
    def _():
        g2[gy] = h_v[...]

    squares = jnp.sum(stream32 * stream32, axis=1, keepdims=True)
    squares = jnp.concatenate([squares, jnp.zeros((TILE - ROWS, 1), F32)], axis=0)
    wide = jnp.broadcast_to(squares, (TILE, TILE))
    sx[0] = jnp.transpose(wide)[0:8, :]

    def sx_copy(d):
        return pltpu.make_async_remote_copy(
            src_ref=sx.at[0],
            dst_ref=sx.at[d],
            send_sem=sx_sem.at[0, d],
            recv_sem=sx_sem.at[1, d],
            device_id=at_x(d),
            device_id_type=MESH,
        )

    def sz_copy(d):
        return pltpu.make_async_remote_copy(
            src_ref=sz.at[0],
            dst_ref=sz.at[d],
            send_sem=sz_sem.at[0, d],
            recv_sem=sz_sem.at[1, d],
            device_id=at_z(d),
            device_id_type=MESH,
        )

    for d in range(1, NX):
        sx_copy(d).start()

    @pl.when(moves)
    def _():
        perm_copy.wait_recv()

    sent = sent + gather(g2, 1)

    for d in range(1, NX):
        sx_copy(d).wait_recv()
    sz[0] = sx[0] + sx[1] + sx[2] + sx[3]
    for d in range(1, NZ):
        sz_copy(d).start()

    for d in range(NY):
        base = 2 * lax.rem(y + d, NY)
        for m in range(4):
            cols = pl.ds(COLS * m, COLS)
            x_other[pl.ds(ROWS * d, ROWS), cols] = g2[4 * (base + 1 - c) + m]
            x_own[pl.ds(ROWS * d, ROWS), cols] = g2[4 * (base + c) + m]
    for copy in wcopy:
        copy.wait()

    def cp_copy(j):
        return pltpu.make_async_remote_copy(
            src_ref=cp_s.at[j],
            dst_ref=cp_r.at[j],
            send_sem=cp_sem.at[0, j],
            recv_sem=cp_sem.at[1, j],
            device_id=partner,
            device_id_type=MESH,
        )

    def y_copy(d, j):
        return pltpu.make_async_remote_copy(
            src_ref=y_s.at[d - 1, j],
            dst_ref=y_r.at[d - 1, j],
            send_sem=ys_sem.at[d - 1, j],
            recv_sem=yr_sem.at[d - 1, j],
            device_id=at_y(d),
            device_id_type=MESH,
        )

    def multiply(j, carry):
        cp_s[j] = jnp.dot(x_other[...], w_v[j], preferred_element_type=F32).astype(BF16)
        cp_copy(j).start()
        own[j] = jnp.dot(x_own[...], w_v[j], preferred_element_type=F32)
        return carry

    def forward(j):
        cp_copy(j).wait_recv()
        for d in (1, 3, 2, 0):
            rows = pl.ds(ROWS * d, ROWS)
            both = own[j, rows, :] + cp_r[j, rows, :].astype(F32)
            if d == 0:
                own[j, rows, :] = both
            else:
                y_s[d - 1, j] = both.astype(BF16)
                y_copy(d, j).start()

    def multiply_forward(j, carry):
        multiply(j, carry)
        forward(j - LAG)
        return carry

    def forward_only(j, carry):
        forward(j)
        return carry

    lax.fori_loop(0, LAG, multiply, 0)
    lax.fori_loop(LAG, CHUNKS, multiply_forward, 0)
    lax.fori_loop(CHUNKS - LAG, CHUNKS, forward_only, 0)

    total = sz[0]
    for d in range(1, NZ):
        sz_copy(d).wait_recv()
        total = total + sz[d]
    tall = jnp.transpose(jnp.broadcast_to(total[0:1, :], (TILE, TILE)))[0:ROWS, :]
    factor = lax.rsqrt(tall / D + norm_eps)

    def finish(j, carry):
        both = own[j, pl.ds(0, ROWS), :]
        for d in (1, 3, 2):
            y_copy(d, j).wait_recv()
            both = both + y_r[d - 1, j].astype(F32)
        gate = both[:, :TILE] * factor
        up = both[:, TILE:] * factor
        cols = pl.ds(pl.multiple_of(j * TILE, TILE), TILE)
        act_v[:, cols] = (gate / (1.0 + jnp.exp(-gate)) * up).astype(BF16)
        return carry

    lax.fori_loop(0, CHUNKS, finish, 0)
    act_out = local(act_v, act_hbm, out_sem.at[1])
    act_out.start()

    for copy in sent:
        copy.wait_send()

    def close_r1(step, carry):
        r1_copy(step).wait_send()
        return carry

    lax.fori_loop(0, NY * NC - 1, close_r1, 0)

    @pl.when(moves)
    def _():
        perm_copy.wait_send()

    for d in range(1, NX):
        sx_copy(d).wait_send()
    for d in range(1, NZ):
        sz_copy(d).wait_send()

    def close_chunk(j, carry):
        cp_copy(j).wait_send()
        for d in (1, 2, 3):
            y_copy(d, j).wait_send()
        return carry

    lax.fori_loop(0, CHUNKS, close_chunk, 0)
    stream_out.wait()
    act_out.wait()


def on_device(
    query,
    cache_key,
    cache_value,
    new_key,
    new_value,
    prefix_len,
    residual,
    out_weight,
    norm_gain,
    gate_weight,
    up_weight,
):
    anywhere = pl.BlockSpec(memory_space=pl.ANY)
    vmem = pltpu.VMEM
    dma = pltpu.SemaphoreType.DMA
    return pl.pallas_call(
        layer_kernel,
        name="decoder_layer",
        out_shape=(
            jax.ShapeDtypeStruct((ROWS, COLS), BF16),
            jax.ShapeDtypeStruct((ROWS, HID), BF16),
        ),
        in_specs=[pl.BlockSpec(memory_space=pltpu.SMEM)] + [anywhere] * 10,
        out_specs=(anywhere, anywhere),
        scratch_shapes=[
            vmem((ROLLS, NEW, GROUP, HD), BF16),
            vmem((ROLLS, CACHE, HD), BF16),
            vmem((ROLLS, CACHE, HD), BF16),
            vmem((ROLLS, NEW, HD), BF16),
            vmem((ROLLS, NEW, HD), BF16),
            vmem((ROWS, COLS), BF16),
            vmem((FEAT, COLS), BF16),
            vmem((D // TILE, TILE), F32),
            vmem((CHUNKS, FEAT, 2 * TILE), BF16),
            vmem((ROLLS * NEW * GROUP, HD), F32),
            vmem((NX * NZ, ROWS, COLS), BF16),
            vmem((NX * NZ, ROWS, COLS), BF16),
            vmem((7, ROWS, COLS), BF16),
            vmem((7, ROWS, COLS), BF16),
            vmem((ROWS, COLS), BF16),
            vmem((ROWS, COLS), BF16),
            vmem((NX, 8, TILE), F32),
            vmem((NZ, 8, TILE), F32),
            vmem((4 * ROWS, FEAT), BF16),
            vmem((4 * ROWS, FEAT), BF16),
            vmem((CHUNKS, 4 * ROWS, 2 * TILE), BF16),
            vmem((CHUNKS, 4 * ROWS, 2 * TILE), BF16),
            vmem((CHUNKS, 4 * ROWS, 2 * TILE), F32),
            vmem((3, CHUNKS, ROWS, 2 * TILE), BF16),
            vmem((3, CHUNKS, ROWS, 2 * TILE), BF16),
            vmem((ROWS, HID), BF16),
            dma((2, ROLLS)),
            dma((6,)),
            dma((2, CHUNKS)),
            dma((2, 62)),
            dma((2, 2, 32)),
            dma((7,)),
            dma((7,)),
            dma((2,)),
            dma((2, NX)),
            dma((2, NZ)),
            dma((2, CHUNKS)),
            dma((3, CHUNKS)),
            dma((3, CHUNKS)),
            dma((2,)),
        ],
        compiler_params=pltpu.CompilerParams(
            collective_id=0, has_side_effects=True, vmem_limit_bytes=50 * 2**20
        ),
    )(
        prefix_len,
        query,
        cache_key,
        cache_value,
        new_key.reshape(ROLLS, NEW, HD),
        new_value.reshape(ROLLS, NEW, HD),
        residual,
        out_weight,
        norm_gain.reshape(D // TILE, TILE),
        gate_weight,
        up_weight,
    )


def solution(mesh):
    in_specs = (
        P(None, None, "gx", None),
        P("gy", "gx", None, None),
        P("gy", "gx", None, None),
        P("gy", None, "gx", None),
        P("gy", None, "gx", None),
        P(),
        P("gx", "gy"),
        P("gx", "gy"),
        P(),
        P("gx", "gy"),
        P("gx", "gy"),
    )
    out_specs = (P("gx", "gy"), P("gx", "gy"))
    return jax.shard_map(
        on_device, mesh=mesh, in_specs=in_specs, out_specs=out_specs, check_vma=False
    )
```

```python
import jax
import jax.numpy as jnp
from jax import lax
from jax.experimental import pallas as pl
from jax.experimental.pallas import tpu as pltpu
from jax.sharding import PartitionSpec as P

MESH = pl.DeviceIdType.MESH
F32 = jnp.float32
BF16 = jnp.bfloat16

NX, NY, NZ, NC = 4, 4, 8, 2
ROLLS = 6
NEW = 4
GROUP = 8
HD = 128
CACHE = 2048
ROWS = 96
COLS = 256
FEAT = 1024
HID = 896
TILE = 128
CHUNKS = HID // TILE
D = 8192
masked_score = -1e30
norm_eps = 1e-05
PER = (24,)
BLOCK = (96,)
FIRST = (0,)
BASE = (0,)
PARTS = len(PER)
SPLIT = ((80, 16),)
LAG = 2
LAG2 = 5
STEP = 2


def layer_kernel(
    len_hbm,
    q_hbm,
    k_hbm,
    v_hbm,
    nk_hbm,
    nv_hbm,
    res_hbm,
    ow_hbm,
    gain_hbm,
    gw_hbm,
    uw_hbm,
    stream_hbm,
    act_hbm,
    len_ref,
    q_v,
    k_v,
    v_v,
    nk_v,
    nv_v,
    res_v,
    ow_v,
    gain_v,
    w_v,
    ho,
    g1,
    g2,
    x_heads,
    p1,
    r1,
    st_v,
    h_v,
    sx,
    sz,
    x_other,
    x_own,
    cp_s,
    cp_r,
    own,
    y_s,
    y_r,
    act_f,
    act_v,
    kv_sem,
    in_sem,
    w_sem,
    ag_send,
    ag_recv,
    agx_recv,
    agz_recv,
    r1_send,
    r1_recv,
    perm_sem,
    sx_sem,
    sz_sem,
    cp_sem,
    ys_sem,
    yr_sem,
    out_sem,
):
    gx = lax.axis_index("gx")
    gy = lax.axis_index("gy")
    y, c = lax.div(gx, NC), lax.rem(gx, NC)
    x, z = lax.div(gy, NZ), lax.rem(gy, NZ)

    xs = [lax.rem(x + d, NX) for d in range(NX)]
    ys = [lax.rem(y + d, NY) for d in range(NY)]
    zs = [lax.rem(z + d, NZ) for d in range(NZ)]
    x_line = [(gx, xx * NZ + z) for xx in xs]
    z_line = [(gx, x * NZ + zz) for zz in zs]

    def at_x(d):
        return x_line[d]

    def at_z(d):
        return z_line[d]

    def at_y(d):
        yy = ys[d] if isinstance(d, int) else lax.rem(y + d, NY)
        return (yy * NC + c, gy)

    partner = (y * NC + 1 - c, gy)
    perm = (lax.div(gy, 4), 4 * gx + lax.rem(gy, 4))
    moves = jnp.logical_or(perm[0] != gx, perm[1] != gy)

    barrier = pltpu.get_barrier_semaphore()

    def greet(device):
        pl.semaphore_signal(barrier, inc=1, device_id=device, device_id_type=MESH)

    for d in range(1, NX):
        greet(at_x(d))
    for d in range(1, NZ):
        greet(at_z(d))
    for d in range(1, NY * NC):
        greet((lax.rem(gx + d, NY * NC), gy))

    @pl.when(moves)
    def _():
        greet(perm)

    def local(src, dst, sem):
        return pltpu.make_async_copy(src, dst, sem)

    small = [
        local(len_hbm, len_ref, in_sem.at[6]),
        local(q_hbm.at[pl.ds(gy * ROLLS, ROLLS)], q_v, in_sem.at[0]),
        local(nk_hbm, nk_v, in_sem.at[1]),
        local(nv_hbm, nv_v, in_sem.at[2]),
    ]
    for copy in small:
        copy.start()
    kcopy = [local(k_hbm.at[r, 0], k_v.at[r], kv_sem.at[0, r]) for r in range(ROLLS)]
    vcopy = [local(v_hbm.at[r, 0], v_v.at[r], kv_sem.at[1, r]) for r in range(ROLLS)]
    for r in range(ROLLS):
        kcopy[r].start()
        vcopy[r].start()
    later = [
        local(ow_hbm, ow_v, in_sem.at[3]),
        local(res_hbm, res_v, in_sem.at[4]),
        local(gain_hbm, gain_v, in_sem.at[5]),
    ]
    for copy in later:
        copy.start()
    wcopy = []
    for j in range(CHUNKS):
        cols = pl.ds(j * TILE, TILE)
        wcopy.append(local(gw_hbm.at[:, cols], w_v.at[j, :, pl.ds(0, TILE)], w_sem.at[0, j]))
        wcopy.append(local(uw_hbm.at[:, cols], w_v.at[j, :, pl.ds(TILE, TILE)], w_sem.at[1, j]))
    for copy in wcopy:
        copy.start()

    closers = []

    def close_all():
        for close in closers:
            close()

    for copy in small:
        copy.wait()
    place = lax.broadcasted_iota(jnp.int32, (NEW * GROUP, CACHE), 1)
    row_id = lax.broadcasted_iota(jnp.int32, (NEW * GROUP, 1), 0)
    scale = HD ** (-0.5)

    def attend(group):
        for r in group:
            kcopy[r].wait()
            vcopy[r].wait()
        for r in group:
            q32 = q_v[r].astype(F32).reshape(NEW * GROUP, HD)
            nk32 = nk_v[r].astype(F32)
            nv32 = nv_v[r].astype(F32)
            scores = (
                lax.dot_general(
                    q32.astype(BF16),
                    k_v[r],
                    (((1,), (1,)), ((), ())),
                    preferred_element_type=F32,
                )
                * scale
            )
            length = len_ref[gy * ROLLS + r]
            scores = jnp.where(place < length, scores, masked_score)
            fresh = []
            for s in range(NEW):
                one = jnp.sum(q32 * nk32[s : s + 1, :], axis=1, keepdims=True) * scale
                fresh.append(jnp.where(row_id >= s * GROUP, one, masked_score))
            top = jnp.max(scores, axis=1, keepdims=True)
            for s in range(NEW):
                top = jnp.maximum(top, fresh[s])
            weights = jnp.exp(scores - top)
            total = jnp.sum(weights, axis=1, keepdims=True)
            mixed = jnp.dot(weights.astype(BF16), v_v[r], preferred_element_type=F32)
            for s in range(NEW):
                weight = jnp.exp(fresh[s] - top)
                total = total + weight
                mixed = mixed + weight.astype(BF16).astype(F32) * nv32[s : s + 1, :]
            ho[pl.ds(r * NEW * GROUP, NEW * GROUP), :] = mixed / total

    for start in range(0, ROLLS, STEP):
        attend(range(start, start + STEP))

    slabs = []
    for q in range(PARTS):
        for slab in range(4):
            parts = [
                ho[pl.ds(8 * 16 * q + 2 * slab + h, PER[q], stride=GROUP), :] for h in range(2)
            ]
            slabs.append(jnp.concatenate(parts, axis=1))
    g1[x, z] = jnp.concatenate(slabs, axis=0).astype(BF16)

    peers = NX - 1 + NZ - 1 + NY * NC - 1

    @pl.when(moves)
    def _():
        pl.semaphore_wait(barrier, peers + 1)

    @pl.when(jnp.logical_not(moves))
    def _():
        pl.semaphore_wait(barrier, peers)

    def gather(ref, phase, first, rows_a, rows_b):
        part_a, part_b = pl.ds(first, rows_a), pl.ds(first + rows_a, rows_b)
        along_z = (1, 7, 2, 6, 3, 5, 4)
        along_x = (1, 3, 2)
        count = [0]

        def send(block, sem, device):
            copy = pltpu.make_async_remote_copy(
                src_ref=block,
                dst_ref=block,
                send_sem=ag_send.at[phase, count[0]],
                recv_sem=sem,
                device_id=device,
                device_id_type=MESH,
            )
            copy.start()
            count[0] += 1
            closers.append(copy.wait_send)

        def piece_a(dx, zz):
            xx = xs[dx]
            return ref.at[xx, zz, part_a], ag_recv.at[phase, xx, zz]

        def piece_b(dx):
            xx = xs[dx]
            return ref.at[xx, z, part_b], agx_recv.at[phase, xx]

        def piece_all(d):
            zz = zs[d]
            return ref.at[:, zz, part_b], agz_recv.at[phase, zz]

        def arrive(block, sem):
            local(block, block, sem).wait()

        for d in along_z:
            send(*piece_a(0, z), at_z(d))
        for d in along_x:
            if rows_b:
                send(*piece_b(0), at_x(d))
        for d in along_x:
            send(*piece_a(0, z), at_x(d))
        yield
        if rows_b:
            for d in along_x:
                arrive(*piece_b(d))
            for d in along_z:
                send(*piece_all(0), at_z(d))
        yield
        for d in along_z:
            piece = piece_a(0, zs[NZ - d])
            arrive(*piece)
            for e in along_x:
                send(*piece, at_x(e))
        yield
        if rows_b:
            for d in along_z:
                arrive(*piece_all(d))
        near = lax.div(z, 4)
        for zz in range(4):
            for d in along_x:
                arrive(*piece_a(d, 4 * near + zz))
        yield
        for zz in range(4):
            for d in along_x:
                arrive(*piece_a(d, 4 * (1 - near) + zz))
        yield

    heads = [gather(g1, q, FIRST[q], *SPLIT[q]) for q in range(PARTS)]
    for step in range(3):
        for q in range(PARTS):
            next(heads[q])

    for copy in later:
        copy.wait()

    def part_of(q):
        return pl.ds(FIRST[q], BLOCK[q])

    def r1_copy(q, n, half, d):
        place = 2 * d + lax.rem(half + c, 2)
        return pltpu.make_async_remote_copy(
            src_ref=p1.at[n, d, part_of(q)],
            dst_ref=r1.at[place, part_of(q)],
            send_sem=r1_send.at[q, n, d],
            recv_sem=r1_recv.at[q, place],
            device_id=(2 * ys[d] + half, gy),
            device_id_type=MESH,
        )

    def project(q, n, half):
        per, size = PER[q], BLOCK[q]
        for d in range(NY):
            got = g1[ys[d], pl.ds(4 * half, 4), part_of(q), :].astype(F32)
            slabs = [
                got[:, per * i : per * i + per, :].reshape(size, COLS) for i in range(4)
            ]
            x_heads[pl.ds(size * d, size), :] = jnp.concatenate(slabs, axis=1).astype(BF16)
        rows = x_heads[pl.ds(0, 4 * size), :]
        part = jnp.dot(rows, ow_v[...], preferred_element_type=F32).astype(BF16)
        for d in (2, 1, 3, 0):
            p1[n, d, part_of(q)] = part[size * d : size * d + size, :]
            if d > 0:
                r1_copy(q, n, half, d).start()
                closers.append(r1_copy(q, n, half, d).wait_send)
        crosses = lax.rem(half + c, 2) == 1

        @pl.when(crosses)
        def _():
            r1_copy(q, n, half, 0).start()

        @pl.when(jnp.logical_not(crosses))
        def _():
            r1[0, part_of(q)] = p1[n, 0, part_of(q)]

        def close():
            @pl.when(crosses)
            def _():
                r1_copy(q, n, half, 0).wait_send()

        closers.append(close)

    near = lax.div(z, 4)

    def project_all(q):
        next(heads[q])
        project(q, 0, near)
        next(heads[q])
        project(q, 1, 1 - near)

    def perm_copy(q):
        return pltpu.make_async_remote_copy(
            src_ref=h_v.at[part_of(q)],
            dst_ref=g2.at[lax.div(perm[1], NZ), lax.rem(perm[1], NZ), part_of(q)],
            send_sem=perm_sem.at[0, q],
            recv_sem=perm_sem.at[1, q],
            device_id=perm,
            device_id_type=MESH,
        )

    def reduce(q):
        residual = res_v[...].astype(F32)
        at, per = 16 * q, PER[q]
        summed = jnp.concatenate(
            [residual[24 * b + at : 24 * b + at + per, :] for b in range(4)], axis=0
        )
        for t in range(NY * NC):
            if t > 0:
                piece = r1.at[t, part_of(q)]
                local(piece, piece, r1_recv.at[q, t]).wait()
            summed = summed + r1[t, part_of(q), :].astype(F32)
        stream32 = summed.astype(BF16).astype(F32)
        h_v[part_of(q), :] = (stream32 * gain).astype(BF16)

        @pl.when(moves)
        def _():
            perm_copy(q).start()

        @pl.when(jnp.logical_not(moves))
        def _():
            g2[x, z, part_of(q)] = h_v[part_of(q), :]

        def close():
            @pl.when(moves)
            def _():
                perm_copy(q).wait_send()

        closers.append(close)
        return stream32

    def arrived(q):
        @pl.when(moves)
        def _():
            perm_copy(q).wait_recv()

    def sx_copy(d):
        return pltpu.make_async_remote_copy(
            src_ref=sx.at[0],
            dst_ref=sx.at[d],
            send_sem=sx_sem.at[0, d],
            recv_sem=sx_sem.at[1, d],
            device_id=at_x(d),
            device_id_type=MESH,
        )

    def sz_copy(d):
        return pltpu.make_async_remote_copy(
            src_ref=sz.at[0],
            dst_ref=sz.at[d],
            send_sem=sz_sem.at[0, d],
            recv_sem=sz_sem.at[1, d],
            device_id=at_z(d),
            device_id_type=MESH,
        )

    gain = jnp.concatenate(
        [gain_v[pl.ds(2 * gy, 1), :], gain_v[pl.ds(2 * gy + 1, 1), :]], axis=1
    )
    rows32 = []
    for q in range(PARTS):
        project_all(q)
    for q in range(PARTS):
        rows32.append(reduce(q))
    halves = [gather(g2, PARTS + q, FIRST[q], *SPLIT[q]) for q in range(PARTS)]
    for q in range(PARTS):
        arrived(q)
        next(halves[q])

    squares = [jnp.sum(rows * rows, axis=1, keepdims=True) for rows in rows32]
    squares = jnp.concatenate(squares + [jnp.zeros((TILE - ROWS, 1), F32)], axis=0)
    sx[0] = jnp.transpose(jnp.broadcast_to(squares, (TILE, TILE)))[0:8, :]
    for d in range(1, NX):
        sx_copy(d).start()
        closers.append(sx_copy(d).wait_send)
    pieces = []
    for b in range(4):
        for q in range(PARTS):
            pieces.append(rows32[q][PER[q] * b : PER[q] * (b + 1), :])
    st_v[...] = jnp.concatenate(pieces, axis=0).astype(BF16)
    stream_out = local(st_v, stream_hbm, out_sem.at[0])
    stream_out.start()
    for step in range(2):
        for q in range(PARTS):
            next(halves[q])
    for d in range(1, NX):
        sx_copy(d).wait_recv()
    sz[0] = sx[0] + sx[1] + sx[2] + sx[3]
    for d in range(1, NZ):
        sz_copy(d).start()
        closers.append(sz_copy(d).wait_send)

    for copy in wcopy:
        copy.wait()

    def core_rows(h):
        return pl.ds(BASE[h], 4 * BLOCK[h])

    def cp_copy(h, j):
        return pltpu.make_async_remote_copy(
            src_ref=cp_s.at[j, core_rows(h)],
            dst_ref=cp_r.at[j, core_rows(h)],
            send_sem=cp_sem.at[0, h, j],
            recv_sem=cp_sem.at[1, h, j],
            device_id=partner,
            device_id_type=MESH,
        )

    def via(h, j):
        return 1 + 2 * lax.rem(j + h, 2)

    def y_copy(h, d, j, to):
        return pltpu.make_async_remote_copy(
            src_ref=y_s.at[d - 1, j, part_of(h)],
            dst_ref=y_r.at[d - 1, j, part_of(h)],
            send_sem=ys_sem.at[h, d - 1, j],
            recv_sem=yr_sem.at[h, d - 1, j],
            device_id=at_y(to),
            device_id_type=MESH,
        )

    def y_rows(h, d):
        return pl.ds(pl.multiple_of(BASE[h] + BLOCK[h] * d, 16), BLOCK[h])

    def run(h):
        size = BLOCK[h]
        for d in range(NY):
            yy = ys[d]
            rows = pl.ds(BASE[h] + size * d, size)
            for m in range(4):
                cols = pl.ds(COLS * m, COLS)
                x_other[rows, cols] = g2[yy, 4 * (1 - c) + m, part_of(h)]
                x_own[rows, cols] = g2[yy, 4 * c + m, part_of(h)]

        def multiply(j):
            other = jnp.dot(x_other[core_rows(h), :], w_v[j], preferred_element_type=F32)
            cp_s[j, core_rows(h)] = other.astype(BF16)
            cp_copy(h, j).start()
            own[j, core_rows(h)] = jnp.dot(
                x_own[core_rows(h), :], w_v[j], preferred_element_type=F32
            )

        def add_cores(j):
            cp_copy(h, j).wait_recv()
            both = own[j, core_rows(h), :] + cp_r[j, core_rows(h), :].astype(F32)
            own[j, core_rows(h)] = both
            y_s[1, j, part_of(h)] = both[2 * size : 3 * size, :].astype(BF16)
            y_copy(h, 2, j, via(h, j)).start()
            direct = 4 - via(h, j)
            y_s[direct - 1, j, part_of(h)] = own[j, y_rows(h, direct), :].astype(BF16)
            y_copy(h, direct, j, direct).start()

        def add_relay(j):
            y_copy(h, 2, j, via(h, j)).wait_recv()
            d = via(h, j)
            both = own[j, y_rows(h, d), :] + y_r[1, j, part_of(h), :].astype(F32)
            y_s[d - 1, j, part_of(h)] = both.astype(BF16)
            y_copy(h, d, j, d).start()

        def step(j, carry):
            @pl.when(j < CHUNKS)
            def _():
                multiply(j)

            @pl.when(jnp.logical_and(j >= LAG, j < CHUNKS + LAG))
            def _():
                add_cores(j - LAG)

            @pl.when(j >= LAG2)
            def _():
                add_relay(j - LAG2)

            return carry

        lax.fori_loop(0, CHUNKS + LAG2, step, 0)

        def close_chunks():
            def close(j, carry):
                cp_copy(h, j).wait_send()
                y_copy(h, 1, j, 1).wait_send()
                y_copy(h, 2, j, via(h, j)).wait_send()
                y_copy(h, 3, j, 3).wait_send()
                return carry

            lax.fori_loop(0, CHUNKS, close, 0)

        closers.append(close_chunks)

    for q in range(PARTS):
        next(halves[q])
        next(halves[q])
        run(q)

    total = sz[0]
    for d in range(1, NZ):
        sz_copy(d).wait_recv()
        total = total + sz[d]
    tall = jnp.transpose(jnp.broadcast_to(total[0:1, :], (TILE, TILE)))[0:ROWS, :]
    factor = lax.rsqrt(tall / D + norm_eps)

    def finish(h):
        size, per = BLOCK[h], PER[h]

        def tile(j, carry):
            both = own[j, pl.ds(BASE[h], size), :]
            for d in (1, 3):
                y_copy(h, d, j, d).wait_recv()
                both = both + y_r[d - 1, j, part_of(h), :].astype(F32)
            here = factor[FIRST[h] : FIRST[h] + size, :]
            gate = both[:, :TILE] * here
            up = both[:, TILE:] * here
            result = gate / (1.0 + jnp.exp(-gate)) * up
            cols = pl.ds(pl.multiple_of(j * TILE, TILE), TILE)
            for b in range(4):
                act_f[pl.ds(24 * b + 16 * h, per), cols] = result[per * b : per * b + per, :]
            return carry

        lax.fori_loop(0, CHUNKS, tile, 0)

    for q in range(PARTS):
        finish(q)
    act_v[...] = act_f[...].astype(BF16)
    act_out = local(act_v, act_hbm, out_sem.at[1])
    act_out.start()
    closers.append(act_out.wait)
    closers.append(stream_out.wait)
    close_all()


def on_device(
    query,
    cache_key,
    cache_value,
    new_key,
    new_value,
    prefix_len,
    residual,
    out_weight,
    norm_gain,
    gate_weight,
    up_weight,
):
    anywhere = pl.BlockSpec(memory_space=pltpu.HBM)
    vmem = pltpu.VMEM
    dma = pltpu.SemaphoreType.DMA
    return pl.pallas_call(
        layer_kernel,
        name="decoder_layer",
        out_shape=(
            jax.ShapeDtypeStruct((ROWS, COLS), BF16),
            jax.ShapeDtypeStruct((ROWS, HID), BF16),
        ),
        in_specs=[anywhere] * 11,
        out_specs=(anywhere, anywhere),
        scratch_shapes=[
            pltpu.SMEM((ROLLS * NX * NZ,), jnp.int32),
            vmem((ROLLS, NEW, GROUP, HD), BF16),
            vmem((ROLLS, CACHE, HD), BF16),
            vmem((ROLLS, CACHE, HD), BF16),
            vmem((ROLLS, NEW, HD), BF16),
            vmem((ROLLS, NEW, HD), BF16),
            vmem((ROWS, COLS), BF16),
            vmem((FEAT, COLS), BF16),
            vmem((D // TILE, TILE), F32),
            vmem((CHUNKS, FEAT, 2 * TILE), BF16),
            vmem((ROLLS * NEW * GROUP, HD), F32),
            vmem((NX, NZ, ROWS, COLS), BF16),
            vmem((NX, NZ, ROWS, COLS), BF16),
            vmem((4 * ROWS, FEAT), BF16),
            vmem((2, NY, ROWS, COLS), BF16),
            vmem((NY * NC, ROWS, COLS), BF16),
            vmem((ROWS, COLS), BF16),
            vmem((ROWS, COLS), BF16),
            vmem((NX, 8, TILE), F32),
            vmem((NZ, 8, TILE), F32),
            vmem((4 * ROWS, FEAT), BF16),
            vmem((4 * ROWS, FEAT), BF16),
            vmem((CHUNKS, 4 * ROWS, 2 * TILE), BF16),
            vmem((CHUNKS, 4 * ROWS, 2 * TILE), BF16),
            vmem((CHUNKS, 4 * ROWS, 2 * TILE), F32),
            vmem((3, CHUNKS, ROWS, 2 * TILE), BF16),
            vmem((3, CHUNKS, ROWS, 2 * TILE), BF16),
            vmem((ROWS, HID), F32),
            vmem((ROWS, HID), BF16),
            dma((2, ROLLS)),
            dma((7,)),
            dma((2, CHUNKS)),
            dma((2 * PARTS, 41)),
            dma((2 * PARTS, NX, NZ)),
            dma((2 * PARTS, NX)),
            dma((2 * PARTS, NZ)),
            dma((2, 2, NY)),
            dma((2, NY * NC)),
            dma((2, 2)),
            dma((2, NX)),
            dma((2, NZ)),
            dma((2, 2, CHUNKS)),
            dma((2, 3, CHUNKS)),
            dma((2, 3, CHUNKS)),
            dma((3,)),
        ],
        compiler_params=pltpu.CompilerParams(
            collective_id=0, has_side_effects=True, vmem_limit_bytes=63 * 2**20
        ),
    )(
        prefix_len,
        query,
        cache_key,
        cache_value,
        new_key.reshape(ROLLS, NEW, HD),
        new_value.reshape(ROLLS, NEW, HD),
        residual,
        out_weight,
        norm_gain.reshape(D // TILE, TILE),
        gate_weight,
        up_weight,
    )


def solution(mesh):
    in_specs = (
        P(None, None, "gx", None),
        P("gy", "gx", None, None),
        P("gy", "gx", None, None),
        P("gy", None, "gx", None),
        P("gy", None, "gx", None),
        P(),
        P("gx", "gy"),
        P("gx", "gy"),
        P(),
        P("gx", "gy"),
        P("gx", "gy"),
    )
    out_specs = (P("gx", "gy"), P("gx", "gy"))
    return jax.shard_map(
        on_device, mesh=mesh, in_specs=in_specs, out_specs=out_specs, check_vma=False
    )
```

```python
import jax
import jax.numpy as jnp
from jax import lax
from jax.experimental import pallas as pl
from jax.experimental.pallas import tpu as pltpu
from jax.sharding import PartitionSpec as P

MESH = pl.DeviceIdType.MESH
F32 = jnp.float32
BF16 = jnp.bfloat16

NX, NY, NZ, NC = 4, 4, 8, 2
ROLLS = 6
NEW = 4
GROUP = 8
HD = 128
CACHE = 2048
ROWS = 96
COLS = 256
FEAT = 1024
HID = 896
TILE = 128
CHUNKS = HID // TILE
D = 8192
masked_score = -1e30
norm_eps = 1e-05
PER = (24,)
BLOCK = (96,)
FIRST = (0,)
BASE = (0,)
PARTS = len(PER)
SPLIT = ((80, 16),)
LAG = 1
LAG2 = 3
STEP = 2


def layer_kernel(
    len_hbm,
    q_hbm,
    k_hbm,
    v_hbm,
    nk_hbm,
    nv_hbm,
    res_hbm,
    ow_hbm,
    gain_hbm,
    gw_hbm,
    uw_hbm,
    stream_hbm,
    act_hbm,
    len_ref,
    q_v,
    k_v,
    v_v,
    nk_v,
    nv_v,
    res_v,
    ow_v,
    gain_v,
    w_v,
    ho,
    g1,
    g2,
    x_heads,
    p1,
    r1,
    st_v,
    h_v,
    sx,
    sz,
    x_other,
    x_own,
    cp_s,
    cp_r,
    own,
    y_s,
    y_r,
    act_f,
    act_v,
    kv_sem,
    in_sem,
    w_sem,
    ag_send,
    ag_recv,
    agx_recv,
    agz_recv,
    r1_send,
    r1_recv,
    perm_sem,
    sx_sem,
    sz_sem,
    cp_sem,
    ys_sem,
    yr_sem,
    out_sem,
):
    gx = lax.axis_index("gx")
    gy = lax.axis_index("gy")
    y, c = lax.div(gx, NC), lax.rem(gx, NC)
    x, z = lax.div(gy, NZ), lax.rem(gy, NZ)

    xs = [lax.rem(x + d, NX) for d in range(NX)]
    ys = [lax.rem(y + d, NY) for d in range(NY)]
    zs = [lax.rem(z + d, NZ) for d in range(NZ)]
    x_line = [(gx, xx * NZ + z) for xx in xs]
    z_line = [(gx, x * NZ + zz) for zz in zs]

    def at_x(d):
        return x_line[d]

    def at_z(d):
        return z_line[d]

    def at_y(d):
        yy = ys[d] if isinstance(d, int) else lax.rem(y + d, NY)
        return (yy * NC + c, gy)

    partner = (y * NC + 1 - c, gy)
    perm = (lax.div(gy, 4), 4 * gx + lax.rem(gy, 4))
    moves = jnp.logical_or(perm[0] != gx, perm[1] != gy)

    barrier = pltpu.get_barrier_semaphore()

    def greet(device):
        pl.semaphore_signal(barrier, inc=1, device_id=device, device_id_type=MESH)

    for d in range(1, NX):
        greet(at_x(d))
    for d in range(1, NZ):
        greet(at_z(d))
    for d in range(1, NY * NC):
        greet((lax.rem(gx + d, NY * NC), gy))

    @pl.when(moves)
    def _():
        greet(perm)

    def local(src, dst, sem):
        return pltpu.make_async_copy(src, dst, sem)

    small = [
        local(len_hbm, len_ref, in_sem.at[6]),
        local(q_hbm.at[pl.ds(gy * ROLLS, ROLLS)], q_v, in_sem.at[0]),
        local(nk_hbm, nk_v, in_sem.at[1]),
        local(nv_hbm, nv_v, in_sem.at[2]),
    ]
    for copy in small:
        copy.start()
    kcopy = [local(k_hbm.at[r, 0], k_v.at[r], kv_sem.at[0, r]) for r in range(ROLLS)]
    vcopy = [local(v_hbm.at[r, 0], v_v.at[r], kv_sem.at[1, r]) for r in range(ROLLS)]
    for r in range(ROLLS):
        kcopy[r].start()
        vcopy[r].start()
    later = [
        local(ow_hbm, ow_v, in_sem.at[3]),
        local(res_hbm, res_v, in_sem.at[4]),
        local(gain_hbm, gain_v, in_sem.at[5]),
    ]
    for copy in later:
        copy.start()
    wcopy = []
    for j in range(CHUNKS):
        cols = pl.ds(j * TILE, TILE)
        wcopy.append(local(gw_hbm.at[:, cols], w_v.at[j, :, pl.ds(0, TILE)], w_sem.at[0, j]))
        wcopy.append(local(uw_hbm.at[:, cols], w_v.at[j, :, pl.ds(TILE, TILE)], w_sem.at[1, j]))
    for copy in wcopy:
        copy.start()

    closers = []

    def close_all():
        for close in closers:
            close()

    for copy in small:
        copy.wait()
    place = lax.broadcasted_iota(jnp.int32, (NEW * GROUP, CACHE), 1)
    row_id = lax.broadcasted_iota(jnp.int32, (NEW * GROUP, 1), 0)
    scale = HD ** (-0.5)

    def attend(group):
        for r in group:
            kcopy[r].wait()
            vcopy[r].wait()
        for r in group:
            q32 = q_v[r].astype(F32).reshape(NEW * GROUP, HD)
            nk32 = nk_v[r].astype(F32)
            nv32 = nv_v[r].astype(F32)
            scores = (
                lax.dot_general(
                    q32.astype(BF16),
                    k_v[r],
                    (((1,), (1,)), ((), ())),
                    preferred_element_type=F32,
                )
                * scale
            )
            length = len_ref[gy * ROLLS + r]
            scores = jnp.where(place < length, scores, masked_score)
            fresh = []
            for s in range(NEW):
                one = jnp.sum(q32 * nk32[s : s + 1, :], axis=1, keepdims=True) * scale
                fresh.append(jnp.where(row_id >= s * GROUP, one, masked_score))
            top = jnp.max(scores, axis=1, keepdims=True)
            for s in range(NEW):
                top = jnp.maximum(top, fresh[s])
            weights = jnp.exp(scores - top)
            total = jnp.sum(weights, axis=1, keepdims=True)
            mixed = jnp.dot(weights.astype(BF16), v_v[r], preferred_element_type=F32)
            for s in range(NEW):
                weight = jnp.exp(fresh[s] - top)
                total = total + weight
                mixed = mixed + weight.astype(BF16).astype(F32) * nv32[s : s + 1, :]
            ho[pl.ds(r * NEW * GROUP, NEW * GROUP), :] = mixed / total

    for start in range(0, ROLLS, STEP):
        attend(range(start, start + STEP))

    slabs = []
    for q in range(PARTS):
        for slab in range(4):
            parts = [
                ho[pl.ds(8 * 16 * q + 2 * slab + h, PER[q], stride=GROUP), :] for h in range(2)
            ]
            slabs.append(jnp.concatenate(parts, axis=1))
    g1[x, z] = jnp.concatenate(slabs, axis=0).astype(BF16)

    peers = NX - 1 + NZ - 1 + NY * NC - 1

    @pl.when(moves)
    def _():
        pl.semaphore_wait(barrier, peers + 1)

    @pl.when(jnp.logical_not(moves))
    def _():
        pl.semaphore_wait(barrier, peers)

    def gather(ref, phase, first, rows_a, rows_b):
        part_a, part_b = pl.ds(first, rows_a), pl.ds(first + rows_a, rows_b)
        along_z = (1, 7, 2, 6, 3, 5, 4)
        along_x = (1, 3, 2)
        count = [0]

        def send(block, sem, device):
            copy = pltpu.make_async_remote_copy(
                src_ref=block,
                dst_ref=block,
                send_sem=ag_send.at[phase, count[0]],
                recv_sem=sem,
                device_id=device,
                device_id_type=MESH,
            )
            copy.start()
            count[0] += 1
            closers.append(copy.wait_send)

        def piece_a(dx, zz):
            xx = xs[dx]
            return ref.at[xx, zz, part_a], ag_recv.at[phase, xx, zz]

        def piece_b(dx):
            xx = xs[dx]
            return ref.at[xx, z, part_b], agx_recv.at[phase, xx]

        def piece_all(d):
            zz = zs[d]
            return ref.at[:, zz, part_b], agz_recv.at[phase, zz]

        def arrive(block, sem):
            local(block, block, sem).wait()

        for d in along_z:
            send(*piece_a(0, z), at_z(d))
        for d in along_x:
            if rows_b:
                send(*piece_b(0), at_x(d))
        for d in along_x:
            send(*piece_a(0, z), at_x(d))
        yield
        if rows_b:
            for d in along_x:
                arrive(*piece_b(d))
            for d in along_z:
                send(*piece_all(0), at_z(d))
        yield
        for d in along_z:
            piece = piece_a(0, zs[NZ - d])
            arrive(*piece)
            for e in along_x:
                send(*piece, at_x(e))
        yield
        if rows_b:
            for d in along_z:
                arrive(*piece_all(d))
        near = lax.div(z, 4)
        for zz in range(4):
            for d in along_x:
                arrive(*piece_a(d, 4 * near + zz))
        yield
        for zz in range(4):
            for d in along_x:
                arrive(*piece_a(d, 4 * (1 - near) + zz))
        yield

    heads = [gather(g1, q, FIRST[q], *SPLIT[q]) for q in range(PARTS)]
    for step in range(3):
        for q in range(PARTS):
            next(heads[q])

    for copy in later:
        copy.wait()

    def part_of(q):
        return pl.ds(FIRST[q], BLOCK[q])

    def r1_copy(q, n, half, d):
        place = 2 * d + lax.rem(half + c, 2)
        return pltpu.make_async_remote_copy(
            src_ref=p1.at[n, d, part_of(q)],
            dst_ref=r1.at[place, part_of(q)],
            send_sem=r1_send.at[q, n, d],
            recv_sem=r1_recv.at[q, place],
            device_id=(2 * ys[d] + half, gy),
            device_id_type=MESH,
        )

    def project(q, n, half):
        per, size = PER[q], BLOCK[q]
        for d in range(NY):
            got = g1[ys[d], pl.ds(4 * half, 4), part_of(q), :].astype(F32)
            slabs = [
                got[:, per * i : per * i + per, :].reshape(size, COLS) for i in range(4)
            ]
            x_heads[pl.ds(size * d, size), :] = jnp.concatenate(slabs, axis=1).astype(BF16)
        rows = x_heads[pl.ds(0, 4 * size), :]
        part = jnp.dot(rows, ow_v[...], preferred_element_type=F32).astype(BF16)
        for d in (2, 1, 3, 0):
            p1[n, d, part_of(q)] = part[size * d : size * d + size, :]
            if d > 0:
                r1_copy(q, n, half, d).start()
                closers.append(r1_copy(q, n, half, d).wait_send)
        crosses = lax.rem(half + c, 2) == 1

        @pl.when(crosses)
        def _():
            r1_copy(q, n, half, 0).start()

        @pl.when(jnp.logical_not(crosses))
        def _():
            r1[0, part_of(q)] = p1[n, 0, part_of(q)]

        def close():
            @pl.when(crosses)
            def _():
                r1_copy(q, n, half, 0).wait_send()

        closers.append(close)

    near = lax.div(z, 4)

    def project_all(q):
        next(heads[q])
        project(q, 0, near)
        next(heads[q])
        project(q, 1, 1 - near)

    def perm_copy(q):
        return pltpu.make_async_remote_copy(
            src_ref=h_v.at[part_of(q)],
            dst_ref=g2.at[lax.div(perm[1], NZ), lax.rem(perm[1], NZ), part_of(q)],
            send_sem=perm_sem.at[0, q],
            recv_sem=perm_sem.at[1, q],
            device_id=perm,
            device_id_type=MESH,
        )

    def reduce(q):
        residual = res_v[...].astype(F32)
        at, per = 16 * q, PER[q]
        summed = jnp.concatenate(
            [residual[24 * b + at : 24 * b + at + per, :] for b in range(4)], axis=0
        )
        for t in range(NY * NC):
            if t > 0:
                piece = r1.at[t, part_of(q)]
                local(piece, piece, r1_recv.at[q, t]).wait()
            summed = summed + r1[t, part_of(q), :].astype(F32)
        stream32 = summed.astype(BF16).astype(F32)
        h_v[part_of(q), :] = (stream32 * gain).astype(BF16)

        @pl.when(moves)
        def _():
            perm_copy(q).start()

        @pl.when(jnp.logical_not(moves))
        def _():
            g2[x, z, part_of(q)] = h_v[part_of(q), :]

        def close():
            @pl.when(moves)
            def _():
                perm_copy(q).wait_send()

        closers.append(close)
        return stream32

    def arrived(q):
        @pl.when(moves)
        def _():
            perm_copy(q).wait_recv()

    def sx_copy(d):
        return pltpu.make_async_remote_copy(
            src_ref=sx.at[0],
            dst_ref=sx.at[d],
            send_sem=sx_sem.at[0, d],
            recv_sem=sx_sem.at[1, d],
            device_id=at_x(d),
            device_id_type=MESH,
        )

    def sz_copy(d):
        return pltpu.make_async_remote_copy(
            src_ref=sz.at[0],
            dst_ref=sz.at[d],
            send_sem=sz_sem.at[0, d],
            recv_sem=sz_sem.at[1, d],
            device_id=at_z(d),
            device_id_type=MESH,
        )

    gain = jnp.concatenate(
        [gain_v[pl.ds(2 * gy, 1), :], gain_v[pl.ds(2 * gy + 1, 1), :]], axis=1
    )
    rows32 = []
    for q in range(PARTS):
        project_all(q)
    for q in range(PARTS):
        rows32.append(reduce(q))
    halves = [gather(g2, PARTS + q, FIRST[q], *SPLIT[q]) for q in range(PARTS)]
    for q in range(PARTS):
        arrived(q)
        next(halves[q])

    squares = [jnp.sum(rows * rows, axis=1, keepdims=True) for rows in rows32]
    squares = jnp.concatenate(squares + [jnp.zeros((TILE - ROWS, 1), F32)], axis=0)
    sx[0] = jnp.transpose(jnp.broadcast_to(squares, (TILE, TILE)))[0:8, :]
    for d in range(1, NX):
        sx_copy(d).start()
        closers.append(sx_copy(d).wait_send)
    pieces = []
    for b in range(4):
        for q in range(PARTS):
            pieces.append(rows32[q][PER[q] * b : PER[q] * (b + 1), :])
    st_v[...] = jnp.concatenate(pieces, axis=0).astype(BF16)
    stream_out = local(st_v, stream_hbm, out_sem.at[0])
    stream_out.start()
    for step in range(2):
        for q in range(PARTS):
            next(halves[q])
    for d in range(1, NX):
        sx_copy(d).wait_recv()
    sz[0] = sx[0] + sx[1] + sx[2] + sx[3]
    for d in range(1, NZ):
        sz_copy(d).start()
        closers.append(sz_copy(d).wait_send)

    for copy in wcopy:
        copy.wait()

    def core_rows(h):
        return pl.ds(BASE[h], 4 * BLOCK[h])

    def cp_copy(h, j):
        return pltpu.make_async_remote_copy(
            src_ref=cp_s.at[j, core_rows(h)],
            dst_ref=cp_r.at[j, core_rows(h)],
            send_sem=cp_sem.at[0, h, j],
            recv_sem=cp_sem.at[1, h, j],
            device_id=partner,
            device_id_type=MESH,
        )

    def via(h, j):
        return 1 + 2 * lax.rem(j + h, 2)

    def y_copy(h, d, j, to):
        return pltpu.make_async_remote_copy(
            src_ref=y_s.at[d - 1, j, part_of(h)],
            dst_ref=y_r.at[d - 1, j, part_of(h)],
            send_sem=ys_sem.at[h, d - 1, j],
            recv_sem=yr_sem.at[h, d - 1, j],
            device_id=at_y(to),
            device_id_type=MESH,
        )

    def y_rows(h, d):
        return pl.ds(pl.multiple_of(BASE[h] + BLOCK[h] * d, 16), BLOCK[h])

    def run(h):
        size = BLOCK[h]
        for d in range(NY):
            yy = ys[d]
            rows = pl.ds(BASE[h] + size * d, size)
            for m in range(4):
                cols = pl.ds(COLS * m, COLS)
                x_other[rows, cols] = g2[yy, 4 * (1 - c) + m, part_of(h)]
                x_own[rows, cols] = g2[yy, 4 * c + m, part_of(h)]

        def multiply(j):
            other = jnp.dot(x_other[core_rows(h), :], w_v[j], preferred_element_type=F32)
            cp_s[j, core_rows(h)] = other.astype(BF16)
            cp_copy(h, j).start()
            own[j, core_rows(h)] = jnp.dot(
                x_own[core_rows(h), :], w_v[j], preferred_element_type=F32
            )

        def add_cores(j):
            cp_copy(h, j).wait_recv()
            both = own[j, core_rows(h), :] + cp_r[j, core_rows(h), :].astype(F32)
            own[j, core_rows(h)] = both
            y_s[1, j, part_of(h)] = both[2 * size : 3 * size, :].astype(BF16)
            y_copy(h, 2, j, via(h, j)).start()
            direct = 4 - via(h, j)
            y_s[direct - 1, j, part_of(h)] = own[j, y_rows(h, direct), :].astype(BF16)
            y_copy(h, direct, j, direct).start()

        def add_relay(j):
            y_copy(h, 2, j, via(h, j)).wait_recv()
            d = via(h, j)
            both = own[j, y_rows(h, d), :] + y_r[1, j, part_of(h), :].astype(F32)
            y_s[d - 1, j, part_of(h)] = both.astype(BF16)
            y_copy(h, d, j, d).start()

        def step(j, carry):
            @pl.when(j < CHUNKS)
            def _():
                multiply(j)

            @pl.when(jnp.logical_and(j >= LAG, j < CHUNKS + LAG))
            def _():
                add_cores(j - LAG)

            @pl.when(j >= LAG2)
            def _():
                add_relay(j - LAG2)

            return carry

        lax.fori_loop(0, CHUNKS + LAG2, step, 0)

        def close_chunks():
            def close(j, carry):
                cp_copy(h, j).wait_send()
                y_copy(h, 1, j, 1).wait_send()
                y_copy(h, 2, j, via(h, j)).wait_send()
                y_copy(h, 3, j, 3).wait_send()
                return carry

            lax.fori_loop(0, CHUNKS, close, 0)

        closers.append(close_chunks)

    for q in range(PARTS):
        next(halves[q])
        next(halves[q])
        run(q)

    total = sz[0]
    for d in range(1, NZ):
        sz_copy(d).wait_recv()
        total = total + sz[d]
    tall = jnp.transpose(jnp.broadcast_to(total[0:1, :], (TILE, TILE)))[0:ROWS, :]
    factor = lax.rsqrt(tall / D + norm_eps)

    def finish(h):
        size, per = BLOCK[h], PER[h]

        def tile(j, carry):
            both = own[j, pl.ds(BASE[h], size), :]
            for d in (1, 3):
                y_copy(h, d, j, d).wait_recv()
                both = both + y_r[d - 1, j, part_of(h), :].astype(F32)
            here = factor[FIRST[h] : FIRST[h] + size, :]
            gate = both[:, :TILE] * here
            up = both[:, TILE:] * here
            result = gate / (1.0 + jnp.exp(-gate)) * up
            cols = pl.ds(pl.multiple_of(j * TILE, TILE), TILE)
            for b in range(4):
                act_f[pl.ds(24 * b + 16 * h, per), cols] = result[per * b : per * b + per, :]
            return carry

        lax.fori_loop(0, CHUNKS, tile, 0)

    for q in range(PARTS):
        finish(q)
    act_v[...] = act_f[...].astype(BF16)
    act_out = local(act_v, act_hbm, out_sem.at[1])
    act_out.start()
    closers.append(act_out.wait)
    closers.append(stream_out.wait)
    close_all()


def on_device(
    query,
    cache_key,
    cache_value,
    new_key,
    new_value,
    prefix_len,
    residual,
    out_weight,
    norm_gain,
    gate_weight,
    up_weight,
):
    anywhere = pl.BlockSpec(memory_space=pltpu.HBM)
    vmem = pltpu.VMEM
    dma = pltpu.SemaphoreType.DMA
    return pl.pallas_call(
        layer_kernel,
        name="decoder_layer",
        out_shape=(
            jax.ShapeDtypeStruct((ROWS, COLS), BF16),
            jax.ShapeDtypeStruct((ROWS, HID), BF16),
        ),
        in_specs=[anywhere] * 11,
        out_specs=(anywhere, anywhere),
        scratch_shapes=[
            pltpu.SMEM((ROLLS * NX * NZ,), jnp.int32),
            vmem((ROLLS, NEW, GROUP, HD), BF16),
            vmem((ROLLS, CACHE, HD), BF16),
            vmem((ROLLS, CACHE, HD), BF16),
            vmem((ROLLS, NEW, HD), BF16),
            vmem((ROLLS, NEW, HD), BF16),
            vmem((ROWS, COLS), BF16),
            vmem((FEAT, COLS), BF16),
            vmem((D // TILE, TILE), F32),
            vmem((CHUNKS, FEAT, 2 * TILE), BF16),
            vmem((ROLLS * NEW * GROUP, HD), F32),
            vmem((NX, NZ, ROWS, COLS), BF16),
            vmem((NX, NZ, ROWS, COLS), BF16),
            vmem((4 * ROWS, FEAT), BF16),
            vmem((2, NY, ROWS, COLS), BF16),
            vmem((NY * NC, ROWS, COLS), BF16),
            vmem((ROWS, COLS), BF16),
            vmem((ROWS, COLS), BF16),
            vmem((NX, 8, TILE), F32),
            vmem((NZ, 8, TILE), F32),
            vmem((4 * ROWS, FEAT), BF16),
            vmem((4 * ROWS, FEAT), BF16),
            vmem((CHUNKS, 4 * ROWS, 2 * TILE), BF16),
            vmem((CHUNKS, 4 * ROWS, 2 * TILE), BF16),
            vmem((CHUNKS, 4 * ROWS, 2 * TILE), F32),
            vmem((3, CHUNKS, ROWS, 2 * TILE), BF16),
            vmem((3, CHUNKS, ROWS, 2 * TILE), BF16),
            vmem((ROWS, HID), F32),
            vmem((ROWS, HID), BF16),
            dma((2, ROLLS)),
            dma((7,)),
            dma((2, CHUNKS)),
            dma((2 * PARTS, 41)),
            dma((2 * PARTS, NX, NZ)),
            dma((2 * PARTS, NX)),
            dma((2 * PARTS, NZ)),
            dma((2, 2, NY)),
            dma((2, NY * NC)),
            dma((2, 2)),
            dma((2, NX)),
            dma((2, NZ)),
            dma((2, 2, CHUNKS)),
            dma((2, 3, CHUNKS)),
            dma((2, 3, CHUNKS)),
            dma((3,)),
        ],
        compiler_params=pltpu.CompilerParams(
            collective_id=0, has_side_effects=True, vmem_limit_bytes=63 * 2**20
        ),
    )(
        prefix_len,
        query,
        cache_key,
        cache_value,
        new_key.reshape(ROLLS, NEW, HD),
        new_value.reshape(ROLLS, NEW, HD),
        residual,
        out_weight,
        norm_gain.reshape(D // TILE, TILE),
        gate_weight,
        up_weight,
    )


def solution(mesh):
    in_specs = (
        P(None, None, "gx", None),
        P("gy", "gx", None, None),
        P("gy", "gx", None, None),
        P("gy", None, "gx", None),
        P("gy", None, "gx", None),
        P(),
        P("gx", "gy"),
        P("gx", "gy"),
        P(),
        P("gx", "gy"),
        P("gx", "gy"),
    )
    out_specs = (P("gx", "gy"), P("gx", "gy"))
    return jax.shard_map(
        on_device, mesh=mesh, in_specs=in_specs, out_specs=out_specs, check_vma=False
    )
```

```python
import jax
import jax.numpy as jnp
from jax import lax
from jax.experimental import pallas as pl
from jax.experimental.pallas import tpu as pltpu
from jax.sharding import PartitionSpec as P

MESH = pl.DeviceIdType.MESH
F32 = jnp.float32
BF16 = jnp.bfloat16

NX, NY, NZ, NC = 4, 4, 8, 2
ROLLS = 6
NEW = 4
GROUP = 8
HD = 128
CACHE = 2048
ROWS = 96
COLS = 256
FEAT = 1024
HID = 896
TILE = 128
CHUNKS = HID // TILE
D = 8192
masked_score = -1e30
norm_eps = 1e-05
PER = (24,)
BLOCK = (96,)
FIRST = (0,)
BASE = (0,)
PARTS = len(PER)
SPLIT = ((80, 16),)
LAG = 1
LAG2 = 3
STEP = 2


def layer_kernel(
    len_hbm,
    q_hbm,
    k_hbm,
    v_hbm,
    nk_hbm,
    nv_hbm,
    res_hbm,
    ow_hbm,
    gain_hbm,
    gw_hbm,
    uw_hbm,
    stream_hbm,
    act_hbm,
    len_ref,
    q_v,
    k_v,
    v_v,
    nk_v,
    nv_v,
    res_v,
    ow_v,
    gain_v,
    w_v,
    ho,
    g1,
    g2,
    x_heads,
    p1,
    r1,
    st_v,
    h_v,
    sx,
    sz,
    x_other,
    x_own,
    cp_s,
    cp_r,
    own,
    y_s,
    y_r,
    act_f,
    act_v,
    kv_sem,
    in_sem,
    w_sem,
    ag_send,
    ag_recv,
    agx_recv,
    agz_recv,
    r1_send,
    r1_recv,
    perm_sem,
    sx_sem,
    sz_sem,
    cp_sem,
    ys_sem,
    yr_sem,
    out_sem,
):
    gx = lax.axis_index("gx")
    gy = lax.axis_index("gy")
    y, c = lax.div(gx, NC), lax.rem(gx, NC)
    x, z = lax.div(gy, NZ), lax.rem(gy, NZ)

    xs = [lax.rem(x + d, NX) for d in range(NX)]
    ys = [lax.rem(y + d, NY) for d in range(NY)]
    zs = [lax.rem(z + d, NZ) for d in range(NZ)]
    x_line = [(gx, xx * NZ + z) for xx in xs]
    z_line = [(gx, x * NZ + zz) for zz in zs]

    def at_x(d):
        return x_line[d]

    def at_z(d):
        return z_line[d]

    def at_y(d):
        yy = ys[d] if isinstance(d, int) else lax.rem(y + d, NY)
        return (yy * NC + c, gy)

    partner = (y * NC + 1 - c, gy)
    perm = (lax.div(gy, 4), 4 * gx + lax.rem(gy, 4))
    moves = jnp.logical_or(perm[0] != gx, perm[1] != gy)

    barrier = pltpu.get_barrier_semaphore()

    def greet(device):
        pl.semaphore_signal(barrier, inc=1, device_id=device, device_id_type=MESH)

    for d in range(1, NX):
        greet(at_x(d))
    for d in range(1, NZ):
        greet(at_z(d))
    for d in range(1, NY * NC):
        greet((lax.rem(gx + d, NY * NC), gy))

    @pl.when(moves)
    def _():
        greet(perm)

    def local(src, dst, sem):
        return pltpu.make_async_copy(src, dst, sem)

    small = [
        local(len_hbm, len_ref, in_sem.at[6]),
        local(q_hbm.at[pl.ds(gy * ROLLS, ROLLS)], q_v, in_sem.at[0]),
        local(nk_hbm, nk_v, in_sem.at[1]),
        local(nv_hbm, nv_v, in_sem.at[2]),
    ]
    for copy in small:
        copy.start()
    kcopy = [local(k_hbm.at[r, 0], k_v.at[r], kv_sem.at[0, r]) for r in range(ROLLS)]
    vcopy = [local(v_hbm.at[r, 0], v_v.at[r], kv_sem.at[1, r]) for r in range(ROLLS)]
    for r in range(ROLLS):
        kcopy[r].start()
        vcopy[r].start()
    later = [
        local(ow_hbm, ow_v, in_sem.at[3]),
        local(res_hbm, res_v, in_sem.at[4]),
        local(gain_hbm, gain_v, in_sem.at[5]),
    ]
    for copy in later:
        copy.start()
    wcopy = []
    for j in range(CHUNKS):
        cols = pl.ds(j * TILE, TILE)
        wcopy.append(local(gw_hbm.at[:, cols], w_v.at[j, :, pl.ds(0, TILE)], w_sem.at[0, j]))
        wcopy.append(local(uw_hbm.at[:, cols], w_v.at[j, :, pl.ds(TILE, TILE)], w_sem.at[1, j]))
    for copy in wcopy:
        copy.start()

    closers = []

    def close_all():
        for close in closers:
            close()

    for copy in small:
        copy.wait()
    place = lax.broadcasted_iota(jnp.int32, (NEW * GROUP, CACHE), 1)
    row_id = lax.broadcasted_iota(jnp.int32, (NEW * GROUP, 1), 0)
    scale = HD ** (-0.5)

    def attend(group):
        for r in group:
            kcopy[r].wait()
            vcopy[r].wait()
        for r in group:
            q32 = q_v[r].astype(F32).reshape(NEW * GROUP, HD)
            nk32 = nk_v[r].astype(F32)
            nv32 = nv_v[r].astype(F32)
            scores = (
                lax.dot_general(
                    q32.astype(BF16),
                    k_v[r],
                    (((1,), (1,)), ((), ())),
                    preferred_element_type=F32,
                )
                * scale
            )
            length = len_ref[gy * ROLLS + r]
            scores = jnp.where(place < length, scores, masked_score)
            fresh = []
            for s in range(NEW):
                one = jnp.sum(q32 * nk32[s : s + 1, :], axis=1, keepdims=True) * scale
                fresh.append(jnp.where(row_id >= s * GROUP, one, masked_score))
            top = jnp.max(scores, axis=1, keepdims=True)
            for s in range(NEW):
                top = jnp.maximum(top, fresh[s])
            weights = jnp.exp(scores - top)
            total = jnp.sum(weights, axis=1, keepdims=True)
            mixed = jnp.dot(weights.astype(BF16), v_v[r], preferred_element_type=F32)
            for s in range(NEW):
                weight = jnp.exp(fresh[s] - top)
                total = total + weight
                mixed = mixed + weight.astype(BF16).astype(F32) * nv32[s : s + 1, :]
            ho[pl.ds(r * NEW * GROUP, NEW * GROUP), :] = mixed / total

    for start in range(0, ROLLS, STEP):
        attend(range(start, start + STEP))

    slabs = []
    for q in range(PARTS):
        for slab in range(4):
            parts = [
                ho[pl.ds(8 * 16 * q + 2 * slab + h, PER[q], stride=GROUP), :] for h in range(2)
            ]
            slabs.append(jnp.concatenate(parts, axis=1))
    g1[x, z] = jnp.concatenate(slabs, axis=0).astype(BF16)

    peers = NX - 1 + NZ - 1 + NY * NC - 1

    @pl.when(moves)
    def _():
        pl.semaphore_wait(barrier, peers + 1)

    @pl.when(jnp.logical_not(moves))
    def _():
        pl.semaphore_wait(barrier, peers)

    def gather(ref, phase, first, rows_a, rows_b):
        part_a, part_b = pl.ds(first, rows_a), pl.ds(first + rows_a, rows_b)
        along_z = (1, 7, 2, 6, 3, 5, 4)
        along_x = (1, 3, 2)
        count = [0]

        def send(block, sem, device):
            copy = pltpu.make_async_remote_copy(
                src_ref=block,
                dst_ref=block,
                send_sem=ag_send.at[phase, count[0]],
                recv_sem=sem,
                device_id=device,
                device_id_type=MESH,
            )
            copy.start()
            count[0] += 1
            closers.append(copy.wait_send)

        def piece_a(dx, zz):
            xx = xs[dx]
            return ref.at[xx, zz, part_a], ag_recv.at[phase, xx, zz]

        def piece_b(dx):
            xx = xs[dx]
            return ref.at[xx, z, part_b], agx_recv.at[phase, xx]

        def piece_all(d):
            zz = zs[d]
            return ref.at[:, zz, part_b], agz_recv.at[phase, zz]

        def arrive(block, sem):
            local(block, block, sem).wait()

        for d in along_z:
            send(*piece_a(0, z), at_z(d))
        for d in along_x:
            if rows_b:
                send(*piece_b(0), at_x(d))
        for d in along_x:
            send(*piece_a(0, z), at_x(d))
        yield
        if rows_b:
            for d in along_x:
                arrive(*piece_b(d))
            for d in along_z:
                send(*piece_all(0), at_z(d))
        yield
        for d in along_z:
            piece = piece_a(0, zs[NZ - d])
            arrive(*piece)
            for e in along_x:
                send(*piece, at_x(e))
        yield
        if rows_b:
            for d in along_z:
                arrive(*piece_all(d))
        near = lax.div(z, 4)
        for zz in range(4):
            for d in along_x:
                arrive(*piece_a(d, 4 * near + zz))
        yield
        for zz in range(4):
            for d in along_x:
                arrive(*piece_a(d, 4 * (1 - near) + zz))
        yield

    heads = [gather(g1, q, FIRST[q], *SPLIT[q]) for q in range(PARTS)]
    for step in range(3):
        for q in range(PARTS):
            next(heads[q])

    for copy in later:
        copy.wait()

    def part_of(q):
        return pl.ds(FIRST[q], BLOCK[q])

    def r1_copy(q, n, half, d):
        place = 2 * d + lax.rem(half + c, 2)
        return pltpu.make_async_remote_copy(
            src_ref=p1.at[n, d, part_of(q)],
            dst_ref=r1.at[place, part_of(q)],
            send_sem=r1_send.at[q, n, d],
            recv_sem=r1_recv.at[q, place],
            device_id=(2 * ys[d] + half, gy),
            device_id_type=MESH,
        )

    def project(q, n, half):
        per, size = PER[q], BLOCK[q]
        for d in range(NY):
            got = g1[ys[d], pl.ds(4 * half, 4), part_of(q), :].astype(F32)
            slabs = [
                got[:, per * i : per * i + per, :].reshape(size, COLS) for i in range(4)
            ]
            x_heads[pl.ds(size * d, size), :] = jnp.concatenate(slabs, axis=1).astype(BF16)
        rows = x_heads[pl.ds(0, 4 * size), :]
        part = jnp.dot(rows, ow_v[...], preferred_element_type=F32).astype(BF16)
        for d in (2, 1, 3, 0):
            p1[n, d, part_of(q)] = part[size * d : size * d + size, :]
            if d > 0:
                r1_copy(q, n, half, d).start()
                closers.append(r1_copy(q, n, half, d).wait_send)
        crosses = lax.rem(half + c, 2) == 1

        @pl.when(crosses)
        def _():
            r1_copy(q, n, half, 0).start()

        @pl.when(jnp.logical_not(crosses))
        def _():
            r1[0, part_of(q)] = p1[n, 0, part_of(q)]

        def close():
            @pl.when(crosses)
            def _():
                r1_copy(q, n, half, 0).wait_send()

        closers.append(close)

    near = lax.div(z, 4)

    def project_all(q):
        next(heads[q])
        project(q, 0, near)
        next(heads[q])
        project(q, 1, 1 - near)

    def perm_copy(q):
        return pltpu.make_async_remote_copy(
            src_ref=h_v.at[part_of(q)],
            dst_ref=g2.at[lax.div(perm[1], NZ), lax.rem(perm[1], NZ), part_of(q)],
            send_sem=perm_sem.at[0, q],
            recv_sem=perm_sem.at[1, q],
            device_id=perm,
            device_id_type=MESH,
        )

    def reduce(q):
        residual = res_v[...].astype(F32)
        at, per = 16 * q, PER[q]
        summed = jnp.concatenate(
            [residual[24 * b + at : 24 * b + at + per, :] for b in range(4)], axis=0
        )
        for t in range(NY * NC):
            if t > 0:
                piece = r1.at[t, part_of(q)]
                local(piece, piece, r1_recv.at[q, t]).wait()
            summed = summed + r1[t, part_of(q), :].astype(F32)
        stream32 = summed.astype(BF16).astype(F32)
        h_v[part_of(q), :] = (stream32 * gain).astype(BF16)

        @pl.when(moves)
        def _():
            perm_copy(q).start()

        @pl.when(jnp.logical_not(moves))
        def _():
            g2[x, z, part_of(q)] = h_v[part_of(q), :]

        def close():
            @pl.when(moves)
            def _():
                perm_copy(q).wait_send()

        closers.append(close)
        return stream32

    def arrived(q):
        @pl.when(moves)
        def _():
            perm_copy(q).wait_recv()

    def sx_copy(d):
        return pltpu.make_async_remote_copy(
            src_ref=sx.at[0],
            dst_ref=sx.at[d],
            send_sem=sx_sem.at[0, d],
            recv_sem=sx_sem.at[1, d],
            device_id=at_x(d),
            device_id_type=MESH,
        )

    def sz_copy(d):
        return pltpu.make_async_remote_copy(
            src_ref=sz.at[0],
            dst_ref=sz.at[d],
            send_sem=sz_sem.at[0, d],
            recv_sem=sz_sem.at[1, d],
            device_id=at_z(d),
            device_id_type=MESH,
        )

    gain = jnp.concatenate(
        [gain_v[pl.ds(2 * gy, 1), :], gain_v[pl.ds(2 * gy + 1, 1), :]], axis=1
    )
    rows32 = []
    for q in range(PARTS):
        project_all(q)
    for q in range(PARTS):
        rows32.append(reduce(q))
    halves = [gather(g2, PARTS + q, FIRST[q], *SPLIT[q]) for q in range(PARTS)]
    for q in range(PARTS):
        arrived(q)
        next(halves[q])

    squares = [jnp.sum(rows * rows, axis=1, keepdims=True) for rows in rows32]
    squares = jnp.concatenate(squares + [jnp.zeros((TILE - ROWS, 1), F32)], axis=0)
    sx[0] = jnp.transpose(jnp.broadcast_to(squares, (TILE, TILE)))[0:8, :]
    for d in range(1, NX):
        sx_copy(d).start()
        closers.append(sx_copy(d).wait_send)
    pieces = []
    for b in range(4):
        for q in range(PARTS):
            pieces.append(rows32[q][PER[q] * b : PER[q] * (b + 1), :])
    st_v[...] = jnp.concatenate(pieces, axis=0).astype(BF16)
    stream_out = local(st_v, stream_hbm, out_sem.at[0])
    stream_out.start()
    for step in range(2):
        for q in range(PARTS):
            next(halves[q])
    for d in range(1, NX):
        sx_copy(d).wait_recv()
    sz[0] = sx[0] + sx[1] + sx[2] + sx[3]
    for d in range(1, NZ):
        sz_copy(d).start()
        closers.append(sz_copy(d).wait_send)

    for copy in wcopy:
        copy.wait()

    def core_rows(h):
        return pl.ds(BASE[h], 4 * BLOCK[h])

    def cp_copy(h, j):
        return pltpu.make_async_remote_copy(
            src_ref=cp_s.at[j, core_rows(h)],
            dst_ref=cp_r.at[j, core_rows(h)],
            send_sem=cp_sem.at[0, h, j],
            recv_sem=cp_sem.at[1, h, j],
            device_id=partner,
            device_id_type=MESH,
        )

    def via(h, j):
        return 1 + 2 * lax.rem(j + h, 2)

    def y_copy(h, d, j, to):
        return pltpu.make_async_remote_copy(
            src_ref=y_s.at[d - 1, j, part_of(h)],
            dst_ref=y_r.at[d - 1, j, part_of(h)],
            send_sem=ys_sem.at[h, d - 1, j],
            recv_sem=yr_sem.at[h, d - 1, j],
            device_id=at_y(to),
            device_id_type=MESH,
        )

    def y_rows(h, d):
        return pl.ds(pl.multiple_of(BASE[h] + BLOCK[h] * d, 16), BLOCK[h])

    def run(h):
        size = BLOCK[h]
        for d in range(NY):
            yy = ys[d]
            rows = pl.ds(BASE[h] + size * d, size)
            for m in range(4):
                cols = pl.ds(COLS * m, COLS)
                x_other[rows, cols] = g2[yy, 4 * (1 - c) + m, part_of(h)]
                x_own[rows, cols] = g2[yy, 4 * c + m, part_of(h)]

        def multiply_other(j, carry):
            other = jnp.dot(x_other[core_rows(h), :], w_v[j], preferred_element_type=F32)
            cp_s[j, core_rows(h)] = other.astype(BF16)
            cp_copy(h, j).start()
            return carry

        def multiply(j):
            own[j, core_rows(h)] = jnp.dot(
                x_own[core_rows(h), :], w_v[j], preferred_element_type=F32
            )

        def add_cores(j):
            cp_copy(h, j).wait_recv()
            both = own[j, core_rows(h), :] + cp_r[j, core_rows(h), :].astype(F32)
            own[j, core_rows(h)] = both
            y_s[1, j, part_of(h)] = both[2 * size : 3 * size, :].astype(BF16)
            y_copy(h, 2, j, via(h, j)).start()
            direct = 4 - via(h, j)
            y_s[direct - 1, j, part_of(h)] = own[j, y_rows(h, direct), :].astype(BF16)
            y_copy(h, direct, j, direct).start()

        def add_relay(j):
            y_copy(h, 2, j, via(h, j)).wait_recv()
            d = via(h, j)
            both = own[j, y_rows(h, d), :] + y_r[1, j, part_of(h), :].astype(F32)
            y_s[d - 1, j, part_of(h)] = both.astype(BF16)
            y_copy(h, d, j, d).start()

        def step(j, carry):
            @pl.when(j < CHUNKS)
            def _():
                multiply(j)

            @pl.when(jnp.logical_and(j >= LAG, j < CHUNKS + LAG))
            def _():
                add_cores(j - LAG)

            @pl.when(j >= LAG2)
            def _():
                add_relay(j - LAG2)

            return carry

        lax.fori_loop(0, CHUNKS, multiply_other, 0)
        lax.fori_loop(0, CHUNKS + LAG2, step, 0)

        def close_chunks():
            def close(j, carry):
                cp_copy(h, j).wait_send()
                y_copy(h, 1, j, 1).wait_send()
                y_copy(h, 2, j, via(h, j)).wait_send()
                y_copy(h, 3, j, 3).wait_send()
                return carry

            lax.fori_loop(0, CHUNKS, close, 0)

        closers.append(close_chunks)

    for q in range(PARTS):
        next(halves[q])
        next(halves[q])
        run(q)

    total = sz[0]
    for d in range(1, NZ):
        sz_copy(d).wait_recv()
        total = total + sz[d]
    tall = jnp.transpose(jnp.broadcast_to(total[0:1, :], (TILE, TILE)))[0:ROWS, :]
    factor = lax.rsqrt(tall / D + norm_eps)

    def finish(h):
        size, per = BLOCK[h], PER[h]

        def tile(j, carry):
            both = own[j, pl.ds(BASE[h], size), :]
            for d in (1, 3):
                y_copy(h, d, j, d).wait_recv()
                both = both + y_r[d - 1, j, part_of(h), :].astype(F32)
            here = factor[FIRST[h] : FIRST[h] + size, :]
            gate = both[:, :TILE] * here
            up = both[:, TILE:] * here
            result = gate / (1.0 + jnp.exp(-gate)) * up
            cols = pl.ds(pl.multiple_of(j * TILE, TILE), TILE)
            for b in range(4):
                act_f[pl.ds(24 * b + 16 * h, per), cols] = result[per * b : per * b + per, :]
            return carry

        lax.fori_loop(0, CHUNKS, tile, 0)

    for q in range(PARTS):
        finish(q)
    act_v[...] = act_f[...].astype(BF16)
    act_out = local(act_v, act_hbm, out_sem.at[1])
    act_out.start()
    closers.append(act_out.wait)
    closers.append(stream_out.wait)
    close_all()


def on_device(
    query,
    cache_key,
    cache_value,
    new_key,
    new_value,
    prefix_len,
    residual,
    out_weight,
    norm_gain,
    gate_weight,
    up_weight,
):
    anywhere = pl.BlockSpec(memory_space=pltpu.HBM)
    vmem = pltpu.VMEM
    dma = pltpu.SemaphoreType.DMA
    return pl.pallas_call(
        layer_kernel,
        name="decoder_layer",
        out_shape=(
            jax.ShapeDtypeStruct((ROWS, COLS), BF16),
            jax.ShapeDtypeStruct((ROWS, HID), BF16),
        ),
        in_specs=[anywhere] * 11,
        out_specs=(anywhere, anywhere),
        scratch_shapes=[
            pltpu.SMEM((ROLLS * NX * NZ,), jnp.int32),
            vmem((ROLLS, NEW, GROUP, HD), BF16),
            vmem((ROLLS, CACHE, HD), BF16),
            vmem((ROLLS, CACHE, HD), BF16),
            vmem((ROLLS, NEW, HD), BF16),
            vmem((ROLLS, NEW, HD), BF16),
            vmem((ROWS, COLS), BF16),
            vmem((FEAT, COLS), BF16),
            vmem((D // TILE, TILE), F32),
            vmem((CHUNKS, FEAT, 2 * TILE), BF16),
            vmem((ROLLS * NEW * GROUP, HD), F32),
            vmem((NX, NZ, ROWS, COLS), BF16),
            vmem((NX, NZ, ROWS, COLS), BF16),
            vmem((4 * ROWS, FEAT), BF16),
            vmem((2, NY, ROWS, COLS), BF16),
            vmem((NY * NC, ROWS, COLS), BF16),
            vmem((ROWS, COLS), BF16),
            vmem((ROWS, COLS), BF16),
            vmem((NX, 8, TILE), F32),
            vmem((NZ, 8, TILE), F32),
            vmem((4 * ROWS, FEAT), BF16),
            vmem((4 * ROWS, FEAT), BF16),
            vmem((CHUNKS, 4 * ROWS, 2 * TILE), BF16),
            vmem((CHUNKS, 4 * ROWS, 2 * TILE), BF16),
            vmem((CHUNKS, 4 * ROWS, 2 * TILE), F32),
            vmem((3, CHUNKS, ROWS, 2 * TILE), BF16),
            vmem((3, CHUNKS, ROWS, 2 * TILE), BF16),
            vmem((ROWS, HID), F32),
            vmem((ROWS, HID), BF16),
            dma((2, ROLLS)),
            dma((7,)),
            dma((2, CHUNKS)),
            dma((2 * PARTS, 41)),
            dma((2 * PARTS, NX, NZ)),
            dma((2 * PARTS, NX)),
            dma((2 * PARTS, NZ)),
            dma((2, 2, NY)),
            dma((2, NY * NC)),
            dma((2, 2)),
            dma((2, NX)),
            dma((2, NZ)),
            dma((2, 2, CHUNKS)),
            dma((2, 3, CHUNKS)),
            dma((2, 3, CHUNKS)),
            dma((3,)),
        ],
        compiler_params=pltpu.CompilerParams(
            collective_id=0, has_side_effects=True, vmem_limit_bytes=63 * 2**20
        ),
    )(
        prefix_len,
        query,
        cache_key,
        cache_value,
        new_key.reshape(ROLLS, NEW, HD),
        new_value.reshape(ROLLS, NEW, HD),
        residual,
        out_weight,
        norm_gain.reshape(D // TILE, TILE),
        gate_weight,
        up_weight,
    )


def solution(mesh):
    in_specs = (
        P(None, None, "gx", None),
        P("gy", "gx", None, None),
        P("gy", "gx", None, None),
        P("gy", None, "gx", None),
        P("gy", None, "gx", None),
        P(),
        P("gx", "gy"),
        P("gx", "gy"),
        P(),
        P("gx", "gy"),
        P("gx", "gy"),
    )
    out_specs = (P("gx", "gy"), P("gx", "gy"))
    return jax.shard_map(
        on_device, mesh=mesh, in_specs=in_specs, out_specs=out_specs, check_vma=False
    )
```
